256 devices in a mesh: dp: 64 (over y_lo, x, z), tensor: 4 (over y_hi, core).
Axes of the slice: x: 4, y: 4 (y_hi: 2, y_lo: 2; y = y_hi * 2 + y_lo), z: 8, core: 2. Of those that a mesh axis runs over, the one named last changes fastest.
Arguments:
- block_out: bfloat16 [65536, 3072], P(('dp', 'tensor')), may hold values from -70 to 70
- gate: float32 [64, 3072], P('dp'), may hold values from -4 to 4
- out_grad: bfloat16 [65536, 3072], P('dp', 'tensor'), may hold values from -8 to 8
- zero_weight: float32 [3072, 3072], P('dp', 'tensor'), may hold values from -0.109375 to 0.109375
- first_moment: float32 [3072, 3072], P('dp', 'tensor'), may hold values from -0.00012 to 0.00012
- second_moment: float32 [3072, 3072], P('dp', 'tensor'), may hold values from 1e-11 to 1e-09
Outputs:
- stream_grad: bfloat16 [65536, 3072], P(('dp', 'tensor'))
- branch_grad: bfloat16 [65536, 3072], P(('dp', 'tensor'))
- zero_step: float32 [3072, 3072], P('dp', 'tensor')
The draws below stay inside these ranges and needn't reach their ends.
All inputs are finite; a program needn't handle non-finite values.
Results may differ from the reference program's by a relative error of at most 0.015.
Values may be sent and summed in bfloat16 or wider, within the bound.
No kernel may reach another device: no remote copies, remote signals or barrier semaphores. Data moves between devices by JAX's collectives and lax.ppermute only.
A program may use at most 128 MiB of HBM per device.

```python
import math
import jax
import jax.numpy as jnp
from jax import lax

D = 3072
TOK = 256
SAMPLES = 64
TOKENS = 65536
N_DP = 64
N_TENSOR = 4


def draw_block_out(key, part):
    key = jax.random.fold_in(key, 11)
    key_scale, key_base = jax.random.split(key, 2)
    column = jnp.arange(D, dtype=jnp.float32) / D
    exponent = 0.5 * column + 0.5 * jax.random.uniform(key_scale, (D,), jnp.float32)
    scales = 10.0 ** exponent
    values = jnp.clip(jax.random.normal(key_base, (TOKENS, D), jnp.float32), -4.0, 4.0) * scales[None, :]
    return values.astype(jnp.bfloat16)


def draw_out_grad(key, part):
    key = jax.random.fold_in(key, 23)
    key_scale, key_base = jax.random.split(key, 2)
    scales = jnp.exp(jax.random.uniform(key_scale, (D,), jnp.float32, jnp.log(0.2), jnp.log(2.0)))
    values = jnp.clip(jax.random.normal(key_base, (TOKENS, D), jnp.float32), -4.0, 4.0) * scales[None, :]
    return values.astype(jnp.bfloat16)


def shard_levels(own_key, dims, cuts, least, high):
    level, own = 1.0, jax.random.fold_in(own_key, 6)
    for position, shards_of in cuts:
        steps = jnp.exp(jax.random.uniform(jax.random.fold_in(own, position), (shards_of,), jnp.float32, least / len(cuts), high / len(cuts)))
        level = level * jnp.repeat(steps, dims[position] // shards_of).reshape([-1 if axis == position else 1 for axis in range(len(dims))])
    return level


def normal_values(stream_key, extent, spread, most, cuts=(), held_as=jnp.bfloat16):
    array = jax.random.normal(stream_key, extent, jnp.float32) * spread
    if len(cuts) > 0:
        array = shard_levels(stream_key, extent, cuts, -0.22, 0.18) * array
    return jnp.clip(array, min=-most, max=most).astype(held_as)


def setup_inputs(seed: int = 0) -> dict:
    keys = jax.random.split(jax.random.key(seed), 7)
    return {
        "block_out": draw_block_out(jax.random.fold_in(keys[6], 71), 0),
        "gate": normal_values(keys[1], (SAMPLES, D), 1.0, 4.0, ((0, 64),), jnp.float32),
        "out_grad": draw_out_grad(jax.random.fold_in(keys[6], 71), 0),
        "zero_weight": normal_values(keys[3], (D, D), D ** -0.5, 0.109375, ((0, 64), (1, 4)), jnp.float32),
        "first_moment": normal_values(keys[4], (D, D), (3e-5), 0.00012, ((0, 64), (1, 4)), jnp.float32),
        "second_moment": jnp.clip(jnp.exp(math.log(9.999999717180685e-10) - 4.6051702 * jax.random.uniform(keys[5], (D, D), jnp.float32) ** shard_levels(keys[5], (D, D), ((0, 64), (1, 4)), -0.2, 0.2)), 9.999999960041972e-12, 9.999999717180685e-10),
    }


beta_one = 0.9
beta_two = 0.999
bias_one = 1.0 - 0.9 ** 10
bias_two = 1.0 - 0.999 ** 10
epsilon = 1e-08
decay_rate = 0.1
max_norm = 1.0

def reference(block_out, gate, out_grad, zero_weight, first_moment, second_moment):
    group_rows = TOK * N_TENSOR
    width_part = D // N_TENSOR
    weight_bf16 = zero_weight.astype(jnp.bfloat16)

    def one_sample(carry, sample):
        start = (sample * group_rows).astype(jnp.int32)
        cotangent = lax.dynamic_slice_in_dim(out_grad, start, group_rows, 0)
        inputs = lax.dynamic_slice_in_dim(block_out, start, group_rows, 0)
        summed = jnp.zeros((group_rows, D), jnp.float32)
        for block in range(N_TENSOR):
            lower = block * width_part
            partial_term = jnp.dot(cotangent[:, lower:lower + width_part], weight_bf16[:, lower:lower + width_part].T, preferred_element_type=jnp.float32)
            rounded = lax.optimization_barrier(partial_term.astype(jnp.bfloat16))
            summed = summed + rounded.astype(jnp.float32)
        gate_row = lax.dynamic_index_in_dim(gate, sample, 0, keepdims=False)
        stream_rows = summed.astype(jnp.bfloat16)
        branch_rows = (gate_row[None, :] * summed).astype(jnp.bfloat16)
        carry = carry + jnp.dot(inputs.T, cotangent, preferred_element_type=jnp.float32)
        return (carry, (stream_rows, branch_rows))
    weight_grad, (stream_all, branch_all) = lax.scan(one_sample, jnp.zeros((D, D), jnp.float32), jnp.arange(N_DP, dtype=jnp.int32))
    stream_grad = stream_all.reshape(N_DP * group_rows, D)
    branch_grad = branch_all.reshape(N_DP * group_rows, D)
    grad_norm = jnp.sqrt(jnp.sum(weight_grad * weight_grad))
    factor = jnp.minimum(1.0, max_norm / (grad_norm + 1e-06))
    clipped = factor * weight_grad
    first = beta_one * first_moment + (1.0 - beta_one) * clipped
    second = beta_two * second_moment + (1.0 - beta_two) * clipped * clipped
    zero_step = first / bias_one / (jnp.sqrt(second / bias_two) + epsilon) + decay_rate * zero_weight
    return (stream_grad, branch_grad, zero_step)
```

```python
import jax
import jax.numpy as jnp
from jax import lax
from jax.experimental import pallas as pl
from jax.experimental.pallas import tpu as pltpu
from jax.sharding import Mesh, PartitionSpec as P

beta_one = 0.9
beta_two = 0.999
bias_one = 1.0 - 0.9**10
bias_two = 1.0 - 0.999**10
epsilon = 1e-08
decay_rate = 0.1
max_norm = 1.0

AXES = ("yl", "x", "z", "yh", "c")
SIZES = (2, 4, 8, 2, 2)
NZ = 8
NXY = 8
OWN = 48
WIDTH = 768
HALF = 384
D = 3072
TOK = 256
F32 = jnp.float32
BF16 = jnp.bfloat16


def index_of(yl, x, z, yh, c):
    return (((yl * 4 + x) * 8 + z) * 2 + yh) * 2 + c


def pairs(move):
    out = []
    for yl in range(2):
        for x in range(4):
            for z in range(8):
                for yh in range(2):
                    for c in range(2):
                        out.append((index_of(yl, x, z, yh, c), index_of(*move(yl, x, z, yh, c))))
    return out


SWAP_CORE = pairs(lambda yl, x, z, yh, c: (yl, x, z, yh, 1 - c))
SWAP_YH = pairs(lambda yl, x, z, yh, c: (yl, x, z, 1 - yh, c))
Z_UP = pairs(lambda yl, x, z, yh, c: (yl, x, (z + 1) % 8, yh, c))
Z_DOWN = pairs(lambda yl, x, z, yh, c: (yl, x, (z - 1) % 8, yh, c))


def send(value, perm):
    return lax.ppermute(value, AXES, perm)


def gather(value, axes, n):
    return lax.all_to_all(jnp.broadcast_to(value[None], (n,) + value.shape), axes, 0, 0, tiled=True)


def gather_ring_z(block, zi):
    half = NXY // 2
    full = jnp.zeros((NXY, NZ) + block.shape[1:], block.dtype)

    def put(full, piece, offset, first=0):
        at = lax.rem(zi + offset + NZ, NZ)
        return lax.dynamic_update_slice(full, piece[:, None], (first, at, 0, 0))

    full = put(full, block, 0)
    up, down = block, block
    for step in range(1, 4):
        up, down = send(up, Z_UP), send(down, Z_DOWN)
        full = put(put(full, up, -step), down, step)
    up, down = send(up[:half], Z_UP), send(down[half:], Z_DOWN)
    return put(put(full, up, 4), down, 4, half)


def scatter_ring_z(parts, zi):
    half = NXY // 2

    def chunk(offset):
        at = lax.rem(zi + offset + NZ, NZ)
        return lax.dynamic_slice_in_dim(parts, at, 1, 1)[:, 0]

    far = chunk(4)
    up, down = send(far[:half], Z_UP), send(far[half:], Z_DOWN)
    here_up, here_down = chunk(3).astype(F32), chunk(-3).astype(F32)
    here_up = jnp.concatenate([here_up[:half] + up.astype(F32), here_up[half:]]).astype(BF16)
    here_down = jnp.concatenate([here_down[:half], here_down[half:] + down.astype(F32)]).astype(BF16)
    for offset in (2, 1):
        up, down = send(here_up, Z_UP), send(here_down, Z_DOWN)
        here_up = (chunk(offset).astype(F32) + up.astype(F32)).astype(BF16)
        here_down = (chunk(-offset).astype(F32) + down.astype(F32)).astype(BF16)
    up, down = send(here_up, Z_UP), send(here_down, Z_DOWN)
    return chunk(0).astype(F32) + up.astype(F32) + down.astype(F32)


def grad_kernel(b0, b1, b2, b3, og, out_a, out_b):
    total = None
    for k, block in enumerate((b0, b1, b2, b3)):
        term = lax.dot_general(
            block[...], og[k * TOK : (k + 1) * TOK, :], (((0,), (0,)), ((), ())), preferred_element_type=F32
        )
        total = term if total is None else total + term
    out_a[...] = total[:, :HALF].astype(BF16)
    out_b[...] = total[:, HALF:].astype(BF16)


def weight_grad(blocks, og):
    tile = 512
    return pl.pallas_call(
        grad_kernel,
        grid=(D // tile,),
        in_specs=[pl.BlockSpec((TOK, tile), lambda i: (0, i))] * 4 + [pl.BlockSpec((4 * TOK, WIDTH), lambda i: (0, 0))],
        out_specs=[pl.BlockSpec((tile, HALF), lambda i: (i, 0))] * 2,
        out_shape=[jax.ShapeDtypeStruct((D, HALF), BF16)] * 2,
        compiler_params=pltpu.CompilerParams(vmem_limit_bytes=40 * 1024 * 1024),
        cost_estimate=pl.CostEstimate(flops=2 * 4 * TOK * WIDTH * D, bytes_accessed=13 * 1024 * 1024, transcendentals=0),
        name="weight_grad",
    )(*blocks, og)


def stream_kernel(og, wa, wb, out):
    total = lax.dot_general(og[:, :HALF], wa[...], (((1,), (1,)), ((), ())), preferred_element_type=F32)
    total += lax.dot_general(og[:, HALF:], wb[...], (((1,), (1,)), ((), ())), preferred_element_type=F32)
    out[...] = total.astype(BF16)


def stream_part(og, wa, wb):
    tile = 768
    return pl.pallas_call(
        stream_kernel,
        grid=(D // tile,),
        in_specs=[
            pl.BlockSpec((TOK, WIDTH), lambda i: (0, 0)),
            pl.BlockSpec((tile, HALF), lambda i: (i, 0)),
            pl.BlockSpec((tile, HALF), lambda i: (i, 0)),
        ],
        out_specs=pl.BlockSpec((TOK, tile), lambda i: (0, i)),
        out_shape=jax.ShapeDtypeStruct((TOK, D), BF16),
        compiler_params=pltpu.CompilerParams(vmem_limit_bytes=40 * 1024 * 1024),
        cost_estimate=pl.CostEstimate(flops=2 * TOK * WIDTH * D, bytes_accessed=7 * 1024 * 1024, transcendentals=0),
        name="stream_part",
    )(og, wa, wb)


def body(block_out, gate, out_grad, zero_weight, first_moment, second_moment):
    zi = lax.axis_index("z")
    ti = lax.axis_index("yh") * 2 + lax.axis_index("c")

    order = [lax.dynamic_slice_in_dim(out_grad, lax.bitwise_xor(ti, k) * TOK, TOK, 0) for k in range(4)]

    with jax.named_scope("block_out"):
        far = send(block_out, SWAP_YH)
        near = send(block_out, SWAP_CORE)
        far_near = send(far, SWAP_CORE)

    weight = zero_weight.astype(BF16)
    with jax.named_scope("weight_gather"):
        rows_a = gather(weight[:, :HALF], ("z",), NZ)
        rows_b = gather(weight[:, HALF:], ("yl", "x"), NXY).reshape(NXY, OWN, HALF)
        weight_a = gather(rows_a, ("yl", "x"), NXY).reshape(D, HALF)
        weight_b = gather_ring_z(rows_b, zi).reshape(D, HALF)

    with jax.named_scope("weight_grad"):
        grad_a, grad_b = weight_grad((block_out, near, far, far_near), jnp.concatenate(order))
        grad_a = grad_a.reshape(NXY, NZ, OWN, HALF)
        grad_b = grad_b.reshape(NXY, NZ, OWN, HALF)

    with jax.named_scope("grad_scatter"):
        got_a = lax.all_to_all(grad_a, ("yl", "x"), 0, 0, tiled=True)
        sum_b = scatter_ring_z(grad_b, zi).astype(BF16)
        sum_a = jnp.sum(got_a.astype(F32), axis=0).astype(BF16)
        got_a = lax.all_to_all(sum_a, ("z",), 0, 0, tiled=True)
        got_b = lax.all_to_all(sum_b, ("yl", "x"), 0, 0, tiled=True)
        own_a = jnp.sum(got_a.astype(F32), axis=0)
        own_b = jnp.sum(got_b.astype(F32), axis=0)
        owner_grad = jnp.concatenate([own_a, own_b], axis=1)

    with jax.named_scope("stream"):
        p3 = stream_part(order[3], weight_a, weight_b)
        r3 = send(p3, SWAP_CORE)
        p2 = stream_part(order[2], weight_a, weight_b)
        s2 = (p2.astype(F32) + r3.astype(F32)).astype(BF16)
        q2 = send(s2, SWAP_YH)
        p1 = stream_part(order[1], weight_a, weight_b)
        r1 = send(p1, SWAP_CORE)
        p0 = stream_part(order[0], weight_a, weight_b)
        stream = p0.astype(F32) + r1.astype(F32) + q2.astype(F32)
        stream_out = stream.astype(BF16)
        branch_out = (gate * stream).astype(BF16)

    with jax.named_scope("norm"):
        local = jnp.sum(owner_grad * owner_grad)
        local = gather(jnp.full((8, 128), local, F32), ("yl", "x", "yh", "c"), 32)
        local = jnp.sum(local, axis=0)
        norm_sq = jnp.sum(gather(local, ("z",), NZ), axis=0)[:1, :1]

    factor = jnp.minimum(1.0, max_norm / (jnp.sqrt(norm_sq) + 1e-06))
    clipped = factor * owner_grad
    first = beta_one * first_moment + (1.0 - beta_one) * clipped
    second = beta_two * second_moment + (1.0 - beta_two) * clipped * clipped
    update = first / bias_one / (jnp.sqrt(second / bias_two) + epsilon) + decay_rate * zero_weight
    return (stream_out, branch_out, update)


def solution(mesh):
    fine = Mesh(mesh.devices.reshape(SIZES), AXES)
    dp, tensor = ("yl", "x", "z"), ("yh", "c")
    placed = (P(AXES, None), P(dp, None), P(dp, tensor), P(dp, tensor), P(dp, tensor), P(dp, tensor))
    return jax.shard_map(
        body,
        mesh=fine,
        in_specs=placed,
        out_specs=(P(AXES, None), P(AXES, None), P(dp, tensor)),
        check_vma=False,
    )
```

```python
import jax
import jax.numpy as jnp
from jax import lax
from jax.experimental import pallas as pl
from jax.experimental.pallas import tpu as pltpu
from jax.sharding import Mesh, PartitionSpec as P

beta_one = 0.9
beta_two = 0.999
bias_one = 1.0 - 0.9**10
bias_two = 1.0 - 0.999**10
epsilon = 1e-08
decay_rate = 0.1
max_norm = 1.0

AXES = ("yl", "x", "z", "yh", "c")
SIZES = (2, 4, 8, 2, 2)
NZ = 8
OWN = 48
WIDTH = 768
D = 3072
TOK = 256
F32 = jnp.float32
BF16 = jnp.bfloat16


def index_of(yl, x, z, yh, c):
    return (((yl * 4 + x) * 8 + z) * 2 + yh) * 2 + c


def pairs(move):
    out = []
    for yl in range(2):
        for x in range(4):
            for z in range(8):
                for yh in range(2):
                    for c in range(2):
                        out.append((index_of(yl, x, z, yh, c), index_of(*move(yl, x, z, yh, c))))
    return out


SWAP_CORE = pairs(lambda yl, x, z, yh, c: (yl, x, z, yh, 1 - c))
SWAP_YH = pairs(lambda yl, x, z, yh, c: (yl, x, z, 1 - yh, c))
SWAP_YL = pairs(lambda yl, x, z, yh, c: (1 - yl, x, z, yh, c))
X_UP = pairs(lambda yl, x, z, yh, c: (yl, (x + 1) % 4, z, yh, c))
X_DOWN = pairs(lambda yl, x, z, yh, c: (yl, (x - 1) % 4, z, yh, c))
X_FAR = pairs(lambda yl, x, z, yh, c: (yl, (x + 2) % 4, z, yh, c))
Z_UP = pairs(lambda yl, x, z, yh, c: (yl, x, (z + 1) % 8, yh, c))
Z_DOWN = pairs(lambda yl, x, z, yh, c: (yl, x, (z - 1) % 8, yh, c))


def send(value, perm):
    return lax.ppermute(value, AXES, perm)


def gather(value, axes, n):
    copies = jnp.broadcast_to(value[None], (n,) + value.shape)
    return lax.all_to_all(copies, axes, 0, 0, tiled=True)


def after(value, *earlier):
    return lax.optimization_barrier((value,) + earlier)[0]


def add(*terms):
    total = terms[0].astype(F32)
    for term in terms[1:]:
        total = total + term.astype(F32)
    return total


VMEM_LIMIT = 28 * 1024 * 1024


def grad_kernel(b0, b1, b2, b3, og, out, blocks):
    for k, block in enumerate((b0, b1, b2, b3)):
        blocks[k * TOK : (k + 1) * TOK, :] = block[...]
    total = lax.dot_general(blocks[...], og[...], (((0,), (0,)), ((), ())), preferred_element_type=F32)
    out[...] = total.astype(BF16)


def weight_grad(blocks, og):
    tile = 768
    return pl.pallas_call(
        grad_kernel,
        grid=(D // tile,),
        in_specs=[pl.BlockSpec((TOK, tile), lambda i: (0, i))] * 4 + [pl.BlockSpec((4 * TOK, WIDTH), lambda i: (0, 0))],
        out_specs=pl.BlockSpec((tile, WIDTH), lambda i: (i, 0)),
        scratch_shapes=[pltpu.VMEM((4 * TOK, tile), BF16)],
        out_shape=jax.ShapeDtypeStruct((D, WIDTH), BF16),
        compiler_params=pltpu.CompilerParams(vmem_limit_bytes=VMEM_LIMIT),
        cost_estimate=pl.CostEstimate(flops=8 * TOK * WIDTH * D, bytes_accessed=16 * 1024 * 1024, transcendentals=0),
        name="weight_grad",
    )(*blocks, og)


def stream_kernel(here, og, *refs):
    blocks, far_low, far_high, (p0, p1, p2, p3, rows) = refs[:7], refs[7], refs[8], refs[9:]
    step = pl.program_id(0)
    yl = lax.rem(step // 2 - here[0] + 2, 2)
    for k in range(2):
        x = lax.rem(lax.rem(step, 2) * 2 + k - here[1] + 4, 4)
        for z, block in zip((0, 1, 2, 3, 5, 6, 7), blocks):
            rows[k, lax.rem(here[2] + z, NZ)] = block[x, yl]
        far = jnp.where(x < 2, far_low[jnp.minimum(x, 1), yl], far_high[jnp.maximum(x - 2, 0), yl])
        rows[k, lax.rem(here[2] + 4, NZ)] = far
    full = rows[...].reshape(2 * NZ * OWN, WIDTH)
    for k, out in enumerate((p0, p1, p2, p3)):
        out[...] = lax.dot_general(
            og[k * TOK : (k + 1) * TOK, :], full, (((1,), (1,)), ((), ())), preferred_element_type=F32
        ).astype(BF16)


def stream_parts(here, og, blocks, far):
    tile = 2 * NZ * OWN
    whole = [pl.BlockSpec((n, 2, OWN, WIDTH), lambda i, here: (0, 0, 0, 0)) for n in (4, 4, 4, 4, 4, 4, 4, 2, 2)]
    return pl.pallas_call(
        stream_kernel,
        grid_spec=pltpu.PrefetchScalarGridSpec(
            num_scalar_prefetch=1,
            grid=(4,),
            in_specs=[pl.BlockSpec((4 * TOK, WIDTH), lambda i, here: (0, 0))] + whole,
            out_specs=[pl.BlockSpec((TOK, tile), lambda i, here: (0, i))] * 4,
            scratch_shapes=[pltpu.VMEM((2, NZ, OWN, WIDTH), BF16)],
        ),
        out_shape=[jax.ShapeDtypeStruct((TOK, D), BF16)] * 4,
        compiler_params=pltpu.CompilerParams(vmem_limit_bytes=VMEM_LIMIT),
        cost_estimate=pl.CostEstimate(flops=8 * TOK * WIDTH * D, bytes_accessed=16 * 1024 * 1024, transcendentals=0),
        name="stream_parts",
    )(here, og, *blocks, *far)


def body(block_out, gate, out_grad, zero_weight, first_moment, second_moment):
    here = jnp.stack([lax.axis_index("yl"), lax.axis_index("x"), lax.axis_index("z")]).astype(jnp.int32)
    ti = lax.axis_index("yh") * 2 + lax.axis_index("c")

    order = [lax.dynamic_slice_in_dim(out_grad, lax.bitwise_xor(ti, k) * TOK, TOK, 0) for k in range(4)]
    out_grad = jnp.concatenate(order)

    with jax.named_scope("start"):
        near = send(block_out, SWAP_CORE)
        weight = zero_weight.astype(BF16)
        other = send(weight, SWAP_YL)
        block_out, other, near = lax.optimization_barrier((block_out, other, near))
        far = send(block_out, SWAP_YH)
        rows = jnp.stack([weight, other])
        x_up, x_down, x_far = send(rows, X_UP), send(rows, X_DOWN), send(rows, X_FAR)
        rows = jnp.stack([rows, x_down, x_far, x_up])

    with jax.named_scope("weight_gather"):
        up, down = send(rows, Z_UP), send(rows, Z_DOWN)
        up, down, far, out_grad = lax.optimization_barrier((up, down, far, out_grad))
        up2, down2 = send(up, Z_UP), send(down, Z_DOWN)

    with jax.named_scope("weight_grad"):
        far_near = send(far, SWAP_CORE)
        grad = weight_grad((block_out, near, far, far_near), out_grad)
        up2, down2 = lax.optimization_barrier((grad, up2, down2))[1:]

    with jax.named_scope("grad_scatter"):
        got = lax.all_to_all(grad.reshape(8, NZ, OWN, WIDTH), ("yl", "x"), 0, 0, tiled=True)

    with jax.named_scope("weight_gather"):
        up3, down3 = send(up2, Z_UP), send(down2, Z_DOWN)
        up3, down3 = lax.optimization_barrier((up3, down3))
        up4, down4 = send(up3[:2], Z_UP), send(down3[2:], Z_DOWN)

    with jax.named_scope("stream"):
        blocks = (rows, down, down2, down3, up3, up2, up)
        p0, p1, p2, p3 = stream_parts(here, out_grad, blocks, (up4, down4))
        r3, r1 = send(p3, SWAP_CORE), send(p1, SWAP_CORE)
        s2 = add(p2, r3).astype(BF16)
        s2, r1 = lax.optimization_barrier((s2, r1))
        q2 = send(s2, SWAP_YH)

    with jax.named_scope("grad_scatter"):
        total = add(*got).astype(BF16)
        owner_grad = add(*lax.all_to_all(total, ("z",), 0, 0, tiled=True))

    with jax.named_scope("norm"):
        local = jnp.sum(owner_grad * owner_grad)
        local = jnp.sum(gather(jnp.full((1, 128), local, F32), ("x", "z"), 32).reshape(32, 128), axis=0, keepdims=True)
        local, q2 = lax.optimization_barrier((local, q2))
        norm_sq = jnp.sum(gather(local, ("yl", "yh", "c"), 8), axis=0)[:1, :1]

    with jax.named_scope("stream"):
        stream = add(p0, r1, q2)
        stream_out = stream.astype(BF16)
        branch_out = (gate * stream).astype(BF16)

    factor = jnp.minimum(1.0, max_norm / (jnp.sqrt(norm_sq) + 1e-06))
    clipped = factor * owner_grad
    first = beta_one * first_moment + (1.0 - beta_one) * clipped
    second = beta_two * second_moment + (1.0 - beta_two) * clipped * clipped
    update = first / bias_one / (jnp.sqrt(second / bias_two) + epsilon) + decay_rate * zero_weight
    return (stream_out, branch_out, update)


def solution(mesh):
    fine = Mesh(mesh.devices.reshape(SIZES), AXES)
    dp, tensor = ("yl", "x", "z"), ("yh", "c")
    placed = (P(AXES, None), P(dp, None), P(dp, tensor), P(dp, tensor), P(dp, tensor), P(dp, tensor))
    return jax.shard_map(
        body,
        mesh=fine,
        in_specs=placed,
        out_specs=(P(AXES, None), P(AXES, None), P(dp, tensor)),
        check_vma=False,
    )
```

```python
import jax
import jax.numpy as jnp
from jax import lax
from jax.experimental import pallas as pl
from jax.experimental.pallas import tpu as pltpu
from jax.sharding import Mesh, PartitionSpec as P

beta_one = 0.9
beta_two = 0.999
bias_one = 1.0 - 0.9**10
bias_two = 1.0 - 0.999**10
epsilon = 1e-08
decay_rate = 0.1
max_norm = 1.0

AXES = ("yl", "x", "z", "yh", "c")
SIZES = (2, 4, 8, 2, 2)
NZ = 8
OWN = 48
WIDTH = 768
D = 3072
TOK = 256
F32 = jnp.float32
BF16 = jnp.bfloat16


def index_of(yl, x, z, yh, c):
    return (((yl * 4 + x) * 8 + z) * 2 + yh) * 2 + c


def pairs(move):
    out = []
    for yl in range(2):
        for x in range(4):
            for z in range(8):
                for yh in range(2):
                    for c in range(2):
                        out.append((index_of(yl, x, z, yh, c), index_of(*move(yl, x, z, yh, c))))
    return out


SWAP_CORE = pairs(lambda yl, x, z, yh, c: (yl, x, z, yh, 1 - c))
SWAP_YH = pairs(lambda yl, x, z, yh, c: (yl, x, z, 1 - yh, c))
SWAP_YL = pairs(lambda yl, x, z, yh, c: (1 - yl, x, z, yh, c))
X_UP = pairs(lambda yl, x, z, yh, c: (yl, (x + 1) % 4, z, yh, c))
X_DOWN = pairs(lambda yl, x, z, yh, c: (yl, (x - 1) % 4, z, yh, c))
X_FAR = pairs(lambda yl, x, z, yh, c: (yl, (x + 2) % 4, z, yh, c))
Z_UP = pairs(lambda yl, x, z, yh, c: (yl, x, (z + 1) % 8, yh, c))
Z_DOWN = pairs(lambda yl, x, z, yh, c: (yl, x, (z - 1) % 8, yh, c))


def send(value, perm):
    return lax.ppermute(value, AXES, perm)


def gather(value, axes, n):
    copies = jnp.broadcast_to(value[None], (n,) + value.shape)
    return lax.all_to_all(copies, axes, 0, 0, tiled=True)


def after(value, *earlier):
    return lax.optimization_barrier((value,) + earlier)[0]


def add(*terms):
    total = terms[0].astype(F32)
    for term in terms[1:]:
        total = total + term.astype(F32)
    return total


VMEM_LIMIT = 28 * 1024 * 1024
ALL_VMEM = 60 * 1024 * 1024


def grad_kernel(b0, b1, b2, b3, og, out, blocks):
    for k, block in enumerate((b0, b1, b2, b3)):
        blocks[k * TOK : (k + 1) * TOK, :] = block[...]
    total = lax.dot_general(blocks[...], og[...], (((0,), (0,)), ((), ())), preferred_element_type=F32)
    out[...] = total.astype(BF16)


def weight_grad(blocks, og):
    tile = 768
    return pl.pallas_call(
        grad_kernel,
        grid=(D // tile,),
        in_specs=[pl.BlockSpec((TOK, tile), lambda i: (0, i))] * 4 + [pl.BlockSpec((4 * TOK, WIDTH), lambda i: (0, 0))],
        out_specs=pl.BlockSpec((tile, WIDTH), lambda i: (i, 0)),
        scratch_shapes=[pltpu.VMEM((4 * TOK, tile), BF16)],
        out_shape=jax.ShapeDtypeStruct((D, WIDTH), BF16),
        compiler_params=pltpu.CompilerParams(vmem_limit_bytes=VMEM_LIMIT),
        cost_estimate=pl.CostEstimate(flops=8 * TOK * WIDTH * D, bytes_accessed=16 * 1024 * 1024, transcendentals=0),
        name="weight_grad",
    )(*blocks, og)


def stream_kernel(here, og, *refs):
    lanes, (p0, p1, p2, p3, rows) = (refs[:9], refs[9:18]), refs[18:]
    step = pl.program_id(0)
    yl = lax.rem(step // 2 - here[0] + 2, 2)
    for lane, blocks in enumerate(lanes):

        @pl.when(yl == lane)
        def _():
            for k in range(2):
                x = lax.rem(lax.rem(step, 2) * 2 + k - here[1] + 4, 4)
                for z, block in zip((0, 1, 2, 3, 5, 6, 7), blocks):
                    rows[k, lax.rem(here[2] + z, NZ)] = block[x]
                far = jnp.where(x < 2, blocks[7][jnp.minimum(x, 1)], blocks[8][jnp.maximum(x - 2, 0)])
                rows[k, lax.rem(here[2] + 4, NZ)] = far

    full = rows[...].reshape(2 * NZ * OWN, WIDTH)
    for k, out in enumerate((p0, p1, p2, p3)):
        out[...] = lax.dot_general(
            og[k * TOK : (k + 1) * TOK, :], full, (((1,), (1,)), ((), ())), preferred_element_type=F32
        ).astype(BF16)


def stream_parts(here, og, blocks):
    tile = 2 * NZ * OWN
    whole = [pl.BlockSpec((n, OWN, WIDTH), lambda i, here: (0, 0, 0)) for n in (4, 4, 4, 4, 4, 4, 4, 2, 2) * 2]
    return pl.pallas_call(
        stream_kernel,
        grid_spec=pltpu.PrefetchScalarGridSpec(
            num_scalar_prefetch=1,
            grid=(4,),
            in_specs=[pl.BlockSpec((4 * TOK, WIDTH), lambda i, here: (0, 0))] + whole,
            out_specs=[pl.BlockSpec((TOK, tile), lambda i, here: (0, i))] * 4,
            scratch_shapes=[pltpu.VMEM((2, NZ, OWN, WIDTH), BF16)],
        ),
        out_shape=[jax.ShapeDtypeStruct((TOK, D), BF16)] * 4,
        compiler_params=pltpu.CompilerParams(vmem_limit_bytes=ALL_VMEM),
        cost_estimate=pl.CostEstimate(flops=8 * TOK * WIDTH * D, bytes_accessed=16 * 1024 * 1024, transcendentals=0),
        name="stream_parts",
    )(here, og, *blocks)


def body(block_out, gate, out_grad, zero_weight, first_moment, second_moment):
    here = jnp.stack([lax.axis_index("yl"), lax.axis_index("x"), lax.axis_index("z")]).astype(jnp.int32)
    ti = lax.axis_index("yh") * 2 + lax.axis_index("c")

    order = [lax.dynamic_slice_in_dim(out_grad, lax.bitwise_xor(ti, k) * TOK, TOK, 0) for k in range(4)]
    out_grad = jnp.concatenate(order)

    with jax.named_scope("start"):
        far = send(block_out, SWAP_YH)
        weight = zero_weight.astype(BF16)
        lane_0 = jnp.stack([weight, send(weight, X_DOWN), send(weight, X_FAR), send(weight, X_UP)])
        near = send(block_out, SWAP_CORE)
        lane_0, near = lax.optimization_barrier((lane_0, near))
        lane_1 = send(lane_0, SWAP_YL)

    def ring(up, down):
        return send(up, Z_UP), send(down, Z_DOWN)

    with jax.named_scope("weight_gather"):
        first_0 = ring(lane_0, lane_0)
        second_0 = ring(*first_0)
        third_0 = ring(*second_0)
        far, out_grad, third_0 = lax.optimization_barrier((far, out_grad, third_0))
        fourth_0 = ring(third_0[0][:2], third_0[1][2:])
        first_1 = ring(lane_1, lane_1)

    with jax.named_scope("weight_grad"):
        far_near = send(far, SWAP_CORE)
        grad = weight_grad((block_out, near, far, far_near), out_grad)

    with jax.named_scope("grad_scatter"):
        got = lax.all_to_all(grad.reshape(8, NZ, OWN, WIDTH), ("yl", "x"), 0, 0, tiled=True)

    with jax.named_scope("weight_gather"):
        first_1, fourth_0 = lax.optimization_barrier((first_1, fourth_0, grad))[:2]
        second_1 = ring(*first_1)
        third_1 = ring(*second_1)
        fourth_1 = ring(third_1[0][:2], third_1[1][2:])

    with jax.named_scope("stream"):
        blocks = []
        for lane, (up, down), (up2, down2), (up3, down3), fourth in (
            (lane_0, first_0, second_0, third_0, fourth_0),
            (lane_1, first_1, second_1, third_1, fourth_1),
        ):
            blocks += [lane, down, down2, down3, up3, up2, up, *fourth]
        p0, p1, p2, p3 = stream_parts(here, out_grad, blocks)
        r3, r1 = send(p3, SWAP_CORE), send(p1, SWAP_CORE)
        s2 = add(p2, r3).astype(BF16)
        s2, r1 = lax.optimization_barrier((s2, r1))
        q2 = send(s2, SWAP_YH)

    with jax.named_scope("grad_scatter"):
        total = add(*got).astype(BF16)
        owner_grad = add(*lax.all_to_all(total, ("z",), 0, 0, tiled=True))

    with jax.named_scope("norm"):
        local = jnp.sum(owner_grad * owner_grad)
        local = gather(jnp.full((1, 128), local, F32), ("x", "z"), 32)
        stream = add(p0, r1, q2)
        stream_out = stream.astype(BF16)
        branch_out = (gate * stream).astype(BF16)
        local, stream_out, branch_out = lax.optimization_barrier((local, stream_out, branch_out))
        local = jnp.sum(local.reshape(32, 128), axis=0, keepdims=True)
        norm_sq = jnp.sum(gather(local, ("yl", "yh", "c"), 8), axis=0)[:1, :1]

    factor = jnp.minimum(1.0, max_norm / (jnp.sqrt(norm_sq) + 1e-06))
    clipped = factor * owner_grad
    first = beta_one * first_moment + (1.0 - beta_one) * clipped
    second = beta_two * second_moment + (1.0 - beta_two) * clipped * clipped
    update = first / bias_one / (jnp.sqrt(second / bias_two) + epsilon) + decay_rate * zero_weight
    return (stream_out, branch_out, update)


def solution(mesh):
    fine = Mesh(mesh.devices.reshape(SIZES), AXES)
    dp, tensor = ("yl", "x", "z"), ("yh", "c")
    placed = (P(AXES, None), P(dp, None), P(dp, tensor), P(dp, tensor), P(dp, tensor), P(dp, tensor))
    return jax.shard_map(
        body,
        mesh=fine,
        in_specs=placed,
        out_specs=(P(AXES, None), P(AXES, None), P(dp, tensor)),
        check_vma=False,
    )
```

```python
import jax
import jax.numpy as jnp
from jax import lax
from jax.experimental import pallas as pl
from jax.experimental.pallas import tpu as pltpu
from jax.sharding import Mesh, PartitionSpec as P

beta_one = 0.9
beta_two = 0.999
bias_one = 1.0 - 0.9**10
bias_two = 1.0 - 0.999**10
epsilon = 1e-08
decay_rate = 0.1
max_norm = 1.0

AXES = ("yl", "xa", "xb", "z", "yh", "c")
SIZES = (2, 2, 2, 8, 2, 2)
NZ = 8
OWN = 48
WIDTH = 768
D = 3072
TOK = 256
F32 = jnp.float32
BF16 = jnp.bfloat16


def index_of(yl, x, z, yh, c):
    return (((yl * 4 + x) * 8 + z) * 2 + yh) * 2 + c


def pairs(move):
    out = []
    for yl in range(2):
        for x in range(4):
            for z in range(8):
                for yh in range(2):
                    for c in range(2):
                        out.append((index_of(yl, x, z, yh, c), index_of(*move(yl, x, z, yh, c))))
    return out


SWAP_CORE = pairs(lambda yl, x, z, yh, c: (yl, x, z, yh, 1 - c))
SWAP_YH = pairs(lambda yl, x, z, yh, c: (yl, x, z, 1 - yh, c))
SWAP_YL = pairs(lambda yl, x, z, yh, c: (1 - yl, x, z, yh, c))
X_UP = pairs(lambda yl, x, z, yh, c: (yl, (x + 1) % 4, z, yh, c))
X_DOWN = pairs(lambda yl, x, z, yh, c: (yl, (x - 1) % 4, z, yh, c))
X_FAR = pairs(lambda yl, x, z, yh, c: (yl, (x + 2) % 4, z, yh, c))
Z_UP = pairs(lambda yl, x, z, yh, c: (yl, x, (z + 1) % 8, yh, c))
Z_DOWN = pairs(lambda yl, x, z, yh, c: (yl, x, (z - 1) % 8, yh, c))


def send(value, perm):
    return lax.ppermute(value, AXES, perm)


def gather(value, axes, n):
    copies = jnp.broadcast_to(value[None], (n,) + value.shape)
    return lax.all_to_all(copies, axes, 0, 0, tiled=True)


def after(value, *earlier):
    return lax.optimization_barrier((value,) + earlier)[0]


def add(*terms):
    total = terms[0].astype(F32)
    for term in terms[1:]:
        total = total + term.astype(F32)
    return total


VMEM_LIMIT = 28 * 1024 * 1024
ALL_VMEM = 60 * 1024 * 1024


def grad_kernel(b0, b1, b2, b3, og, out, blocks):
    for k, block in enumerate((b0, b1, b2, b3)):
        blocks[k * TOK : (k + 1) * TOK, :] = block[...]
    total = lax.dot_general(blocks[...], og[...], (((0,), (0,)), ((), ())), preferred_element_type=F32)
    out[...] = total.astype(BF16).reshape(2, 1, 1, NZ, OWN, WIDTH)


def weight_grad(blocks, og):
    tile = 768
    return pl.pallas_call(
        grad_kernel,
        grid=(D // tile,),
        in_specs=[pl.BlockSpec((TOK, tile), lambda i: (0, i))] * 4 + [pl.BlockSpec((4 * TOK, WIDTH), lambda i: (0, 0))],
        out_specs=pl.BlockSpec((2, 1, 1, NZ, OWN, WIDTH), lambda i: (0, lax.rem(i, 2), i // 2, 0, 0, 0)),
        scratch_shapes=[pltpu.VMEM((4 * TOK, tile), BF16)],
        out_shape=jax.ShapeDtypeStruct((2, 2, 2, NZ, OWN, WIDTH), BF16),
        compiler_params=pltpu.CompilerParams(vmem_limit_bytes=VMEM_LIMIT),
        cost_estimate=pl.CostEstimate(flops=8 * TOK * WIDTH * D, bytes_accessed=16 * 1024 * 1024, transcendentals=0),
        name="weight_grad",
    )(*blocks, og)


def stream_kernel(here, og, *refs):
    lanes, (p0, p1, p2, p3, rows) = (refs[:9], refs[9:18]), refs[18:]
    step = pl.program_id(0)
    yl = lax.rem(step // 2 - here[0] + 2, 2)
    for lane, blocks in enumerate(lanes):

        @pl.when(yl == lane)
        def _():
            for k in range(2):
                x = lax.rem(lax.rem(step, 2) * 2 + k - here[1] + 4, 4)
                for z, block in zip((0, 1, 2, 3, 5, 6, 7), blocks):
                    rows[k, lax.rem(here[2] + z, NZ)] = block[x]
                far = jnp.where(x < 2, blocks[7][jnp.minimum(x, 1)], blocks[8][jnp.maximum(x - 2, 0)])
                rows[k, lax.rem(here[2] + 4, NZ)] = far

    full = rows[...].reshape(2 * NZ * OWN, WIDTH)
    for k, out in enumerate((p0, p1, p2, p3)):
        out[...] = lax.dot_general(
            og[k * TOK : (k + 1) * TOK, :], full, (((1,), (1,)), ((), ())), preferred_element_type=F32
        ).astype(BF16)


def stream_parts(here, og, blocks):
    tile = 2 * NZ * OWN
    whole = [pl.BlockSpec((n, OWN, WIDTH), lambda i, here: (0, 0, 0)) for n in (4, 4, 4, 4, 4, 4, 4, 2, 2) * 2]
    return pl.pallas_call(
        stream_kernel,
        grid_spec=pltpu.PrefetchScalarGridSpec(
            num_scalar_prefetch=1,
            grid=(4,),
            in_specs=[pl.BlockSpec((4 * TOK, WIDTH), lambda i, here: (0, 0))] + whole,
            out_specs=[pl.BlockSpec((TOK, tile), lambda i, here: (0, i))] * 4,
            scratch_shapes=[pltpu.VMEM((2, NZ, OWN, WIDTH), BF16)],
        ),
        out_shape=[jax.ShapeDtypeStruct((TOK, D), BF16)] * 4,
        compiler_params=pltpu.CompilerParams(vmem_limit_bytes=ALL_VMEM),
        cost_estimate=pl.CostEstimate(flops=8 * TOK * WIDTH * D, bytes_accessed=16 * 1024 * 1024, transcendentals=0),
        name="stream_parts",
    )(here, og, *blocks)


def body(block_out, gate, out_grad, zero_weight, first_moment, second_moment):
    here = jnp.stack([lax.axis_index("yl"), lax.axis_index(("xa", "xb")), lax.axis_index("z")]).astype(jnp.int32)
    ti = lax.axis_index("yh") * 2 + lax.axis_index("c")

    order = [lax.dynamic_slice_in_dim(out_grad, lax.bitwise_xor(ti, k) * TOK, TOK, 0) for k in range(4)]
    out_grad = jnp.concatenate(order)

    with jax.named_scope("start"):
        far = send(block_out, SWAP_YH)
        weight = zero_weight.astype(BF16)
        lane_0 = jnp.stack([weight, send(weight, X_DOWN), send(weight, X_FAR), send(weight, X_UP)])
        near = send(block_out, SWAP_CORE)
        lane_0, near = lax.optimization_barrier((lane_0, near))
        lane_1 = send(lane_0, SWAP_YL)

    def ring(up, down):
        return send(up, Z_UP), send(down, Z_DOWN)

    with jax.named_scope("weight_gather"):
        first_0 = ring(lane_0, lane_0)
        second_0 = ring(*first_0)
        third_0 = ring(*second_0)
        far, out_grad, third_0 = lax.optimization_barrier((far, out_grad, third_0))
        fourth_0 = ring(third_0[0][:2], third_0[1][2:])
        first_1 = ring(lane_1, lane_1)

    with jax.named_scope("weight_grad"):
        far_near = send(far, SWAP_CORE)
        grad = weight_grad((block_out, near, far, far_near), out_grad)

    with jax.named_scope("grad_scatter"):
        got = lax.all_to_all(grad.reshape(8, NZ, OWN, WIDTH), ("xb", "xa", "yl"), 0, 0, tiled=True)

    with jax.named_scope("weight_gather"):
        first_1, fourth_0 = lax.optimization_barrier((first_1, fourth_0, grad))[:2]
        second_1 = ring(*first_1)
        third_1 = ring(*second_1)
        fourth_1 = ring(third_1[0][:2], third_1[1][2:])

    with jax.named_scope("stream"):
        blocks = []
        for lane, (up, down), (up2, down2), (up3, down3), fourth in (
            (lane_0, first_0, second_0, third_0, fourth_0),
            (lane_1, first_1, second_1, third_1, fourth_1),
        ):
            blocks += [lane, down, down2, down3, up3, up2, up, *fourth]
        p0, p1, p2, p3 = stream_parts(here, out_grad, blocks)
        r3, r1 = send(p3, SWAP_CORE), send(p1, SWAP_CORE)
        s2 = add(p2, r3).astype(BF16)
        s2, r1 = lax.optimization_barrier((s2, r1))
        q2 = send(s2, SWAP_YH)

    with jax.named_scope("grad_scatter"):
        total = add(*got).astype(BF16)
        owner_grad = add(*lax.all_to_all(total, ("z",), 0, 0, tiled=True))

    with jax.named_scope("norm"):
        local = jnp.sum(owner_grad * owner_grad)
        local = gather(jnp.full((1, 128), local, F32), ("xa", "xb", "z"), 32)
        stream = add(p0, r1, q2)
        stream_out = stream.astype(BF16)
        branch_out = (gate * stream).astype(BF16)
        local, stream_out, branch_out = lax.optimization_barrier((local, stream_out, branch_out))
        local = jnp.sum(local.reshape(32, 128), axis=0, keepdims=True)
        norm_sq = jnp.sum(gather(local, ("yl", "yh", "c"), 8), axis=0)[:1, :1]

    factor = jnp.minimum(1.0, max_norm / (jnp.sqrt(norm_sq) + 1e-06))
    clipped = factor * owner_grad
    first = beta_one * first_moment + (1.0 - beta_one) * clipped
    second = beta_two * second_moment + (1.0 - beta_two) * clipped * clipped
    update = first / bias_one / (jnp.sqrt(second / bias_two) + epsilon) + decay_rate * zero_weight
    return (stream_out, branch_out, update)


def solution(mesh):
    fine = Mesh(mesh.devices.reshape(SIZES), AXES)
    dp, tensor = ("yl", "xa", "xb", "z"), ("yh", "c")
    placed = (P(AXES, None), P(dp, None), P(dp, tensor), P(dp, tensor), P(dp, tensor), P(dp, tensor))
    return jax.shard_map(
        body,
        mesh=fine,
        in_specs=placed,
        out_specs=(P(AXES, None), P(AXES, None), P(dp, tensor)),
        check_vma=False,
    )
```

```python
import jax
import jax.numpy as jnp
from jax import lax
from jax.experimental import pallas as pl
from jax.experimental.pallas import tpu as pltpu
from jax.sharding import Mesh, PartitionSpec as P

beta_one = 0.9
beta_two = 0.999
bias_one = 1.0 - 0.9**10
bias_two = 1.0 - 0.999**10
epsilon = 1e-08
decay_rate = 0.1
max_norm = 1.0

AXES = ("yl", "xa", "xb", "z", "yh", "c")
SIZES = (2, 2, 2, 8, 2, 2)
NZ = 8
OWN = 48
WIDTH = 768
D = 3072
TOK = 256
F32 = jnp.float32
BF16 = jnp.bfloat16


def index_of(yl, x, z, yh, c):
    return (((yl * 4 + x) * 8 + z) * 2 + yh) * 2 + c


def pairs(move):
    out = []
    for yl in range(2):
        for x in range(4):
            for z in range(8):
                for yh in range(2):
                    for c in range(2):
                        out.append((index_of(yl, x, z, yh, c), index_of(*move(yl, x, z, yh, c))))
    return out


SWAP_CORE = pairs(lambda yl, x, z, yh, c: (yl, x, z, yh, 1 - c))
SWAP_YH = pairs(lambda yl, x, z, yh, c: (yl, x, z, 1 - yh, c))
SWAP_YL = pairs(lambda yl, x, z, yh, c: (1 - yl, x, z, yh, c))
X_UP = pairs(lambda yl, x, z, yh, c: (yl, (x + 1) % 4, z, yh, c))
X_DOWN = pairs(lambda yl, x, z, yh, c: (yl, (x - 1) % 4, z, yh, c))
X_FAR = pairs(lambda yl, x, z, yh, c: (yl, (x + 2) % 4, z, yh, c))
Z_UP = pairs(lambda yl, x, z, yh, c: (yl, x, (z + 1) % 8, yh, c))
Z_DOWN = pairs(lambda yl, x, z, yh, c: (yl, x, (z - 1) % 8, yh, c))


def send(value, perm):
    return lax.ppermute(value, AXES, perm)


def gather(value, axes, n):
    copies = jnp.broadcast_to(value[None], (n,) + value.shape)
    return lax.all_to_all(copies, axes, 0, 0, tiled=True)


def after(value, *earlier):
    return lax.optimization_barrier((value,) + earlier)[0]


def add(*terms):
    total = terms[0].astype(F32)
    for term in terms[1:]:
        total = total + term.astype(F32)
    return total


VMEM_LIMIT = 28 * 1024 * 1024
ALL_VMEM = 60 * 1024 * 1024


def grad_kernel(b0, b1, b2, b3, og, out, blocks):
    for k, block in enumerate((b0, b1, b2, b3)):
        blocks[k * TOK : (k + 1) * TOK, :] = block[...]
    total = lax.dot_general(blocks[...], og[...], (((0,), (0,)), ((), ())), preferred_element_type=F32)
    out[...] = total.astype(BF16).reshape(2, 1, 1, NZ, OWN, WIDTH)


def weight_grad(blocks, og):
    tile = 768
    return pl.pallas_call(
        grad_kernel,
        grid=(D // tile,),
        in_specs=[pl.BlockSpec((TOK, tile), lambda i: (0, i))] * 4 + [pl.BlockSpec((4 * TOK, WIDTH), lambda i: (0, 0))],
        out_specs=pl.BlockSpec((2, 1, 1, NZ, OWN, WIDTH), lambda i: (0, i // 2, lax.rem(i, 2), 0, 0, 0)),
        scratch_shapes=[pltpu.VMEM((4 * TOK, tile), BF16)],
        out_shape=jax.ShapeDtypeStruct((2, 2, 2, NZ, OWN, WIDTH), BF16),
        compiler_params=pltpu.CompilerParams(vmem_limit_bytes=VMEM_LIMIT),
        cost_estimate=pl.CostEstimate(flops=8 * TOK * WIDTH * D, bytes_accessed=16 * 1024 * 1024, transcendentals=0),
        name="weight_grad",
    )(*blocks, og)


def stream_kernel(here, og, *refs):
    lanes, (p0, p1, p2, p3, rows) = (refs[:9], refs[9:18]), refs[18:]
    step = pl.program_id(0)
    yl = lax.rem(step // 2 - here[0] + 2, 2)
    for lane, blocks in enumerate(lanes):

        @pl.when(yl == lane)
        def _():
            for k in range(2):
                x = lax.rem(lax.rem(step, 2) * 2 + k - here[1] + 4, 4)
                for z, block in zip((0, 1, 2, 3, 5, 6, 7), blocks):
                    rows[k, lax.rem(here[2] + z, NZ)] = block[x]
                far = jnp.where(x < 2, blocks[7][jnp.minimum(x, 1)], blocks[8][jnp.maximum(x - 2, 0)])
                rows[k, lax.rem(here[2] + 4, NZ)] = far

    full = rows[...].reshape(2 * NZ * OWN, WIDTH)
    for k, out in enumerate((p0, p1, p2, p3)):
        out[...] = lax.dot_general(
            og[k * TOK : (k + 1) * TOK, :], full, (((1,), (1,)), ((), ())), preferred_element_type=F32
        ).astype(BF16)


def stream_parts(here, og, blocks):
    tile = 2 * NZ * OWN
    whole = [pl.BlockSpec((n, OWN, WIDTH), lambda i, here: (0, 0, 0)) for n in (4, 4, 4, 4, 4, 4, 4, 2, 2) * 2]
    return pl.pallas_call(
        stream_kernel,
        grid_spec=pltpu.PrefetchScalarGridSpec(
            num_scalar_prefetch=1,
            grid=(4,),
            in_specs=[pl.BlockSpec((4 * TOK, WIDTH), lambda i, here: (0, 0))] + whole,
            out_specs=[pl.BlockSpec((TOK, tile), lambda i, here: (0, i))] * 4,
            scratch_shapes=[pltpu.VMEM((2, NZ, OWN, WIDTH), BF16)],
        ),
        out_shape=[jax.ShapeDtypeStruct((TOK, D), BF16)] * 4,
        compiler_params=pltpu.CompilerParams(vmem_limit_bytes=ALL_VMEM),
        cost_estimate=pl.CostEstimate(flops=8 * TOK * WIDTH * D, bytes_accessed=16 * 1024 * 1024, transcendentals=0),
        name="stream_parts",
    )(here, og, *blocks)


def body(block_out, gate, out_grad, zero_weight, first_moment, second_moment):
    here = jnp.stack([lax.axis_index("yl"), lax.axis_index(("xa", "xb")), lax.axis_index("z")]).astype(jnp.int32)
    ti = lax.axis_index("yh") * 2 + lax.axis_index("c")

    order = [lax.dynamic_slice_in_dim(out_grad, lax.bitwise_xor(ti, k) * TOK, TOK, 0) for k in range(4)]
    out_grad = jnp.concatenate(order)

    with jax.named_scope("start"):
        far = send(block_out, SWAP_YH)
        weight = zero_weight.astype(BF16)
        lane_0 = jnp.stack([weight, send(weight, X_DOWN), send(weight, X_FAR), send(weight, X_UP)])
        near = send(block_out, SWAP_CORE)
        lane_0, near = lax.optimization_barrier((lane_0, near))
        lane_1 = send(lane_0, SWAP_YL)

    def ring(up, down):
        return send(up, Z_UP), send(down, Z_DOWN)

    with jax.named_scope("weight_gather"):
        first_0 = ring(lane_0, lane_0)
        second_0 = ring(*first_0)
        third_0 = ring(*second_0)
        far, out_grad, third_0 = lax.optimization_barrier((far, out_grad, third_0))
        fourth_0 = ring(third_0[0][:2], third_0[1][2:])
        first_1 = ring(lane_1, lane_1)

    with jax.named_scope("weight_grad"):
        far_near = send(far, SWAP_CORE)
        grad = weight_grad((block_out, near, far, far_near), out_grad)

    with jax.named_scope("grad_scatter"):
        got = lax.all_to_all(grad.reshape(8, NZ, OWN, WIDTH), ("xb", "yl", "xa"), 0, 0, tiled=True)

    with jax.named_scope("weight_gather"):
        first_1, fourth_0 = lax.optimization_barrier((first_1, fourth_0, grad))[:2]
        second_1 = ring(*first_1)
        third_1 = ring(*second_1)
        fourth_1 = ring(third_1[0][:2], third_1[1][2:])

    with jax.named_scope("stream"):
        blocks = []
        for lane, (up, down), (up2, down2), (up3, down3), fourth in (
            (lane_0, first_0, second_0, third_0, fourth_0),
            (lane_1, first_1, second_1, third_1, fourth_1),
        ):
            blocks += [lane, down, down2, down3, up3, up2, up, *fourth]
        p0, p1, p2, p3 = stream_parts(here, out_grad, blocks)
        r3, r1 = send(p3, SWAP_CORE), send(p1, SWAP_CORE)
        s2 = add(p2, r3).astype(BF16)
        s2, r1 = lax.optimization_barrier((s2, r1))
        q2 = send(s2, SWAP_YH)

    with jax.named_scope("grad_scatter"):
        total = add(*got).astype(BF16)
        owner_grad = add(*lax.all_to_all(total, ("z",), 0, 0, tiled=True))

    with jax.named_scope("norm"):
        local = jnp.sum(owner_grad * owner_grad)
        local = gather(jnp.full((1, 128), local, F32), ("xa", "xb", "z"), 32)
        stream = add(p0, r1, q2)
        stream_out = stream.astype(BF16)
        branch_out = (gate * stream).astype(BF16)
        local, stream_out, branch_out = lax.optimization_barrier((local, stream_out, branch_out))
        local = jnp.sum(local.reshape(32, 128), axis=0, keepdims=True)
        norm_sq = jnp.sum(gather(local, ("yl", "yh", "c"), 8), axis=0)[:1, :1]

    factor = jnp.minimum(1.0, max_norm / (jnp.sqrt(norm_sq) + 1e-06))
    clipped = factor * owner_grad
    first = beta_one * first_moment + (1.0 - beta_one) * clipped
    second = beta_two * second_moment + (1.0 - beta_two) * clipped * clipped
    update = first / bias_one / (jnp.sqrt(second / bias_two) + epsilon) + decay_rate * zero_weight
    return (stream_out, branch_out, update)


def solution(mesh):
    fine = Mesh(mesh.devices.reshape(SIZES), AXES)
    dp, tensor = ("yl", "xa", "xb", "z"), ("yh", "c")
    placed = (P(AXES, None), P(dp, None), P(dp, tensor), P(dp, tensor), P(dp, tensor), P(dp, tensor))
    return jax.shard_map(
        body,
        mesh=fine,
        in_specs=placed,
        out_specs=(P(AXES, None), P(AXES, None), P(dp, tensor)),
        check_vma=False,
    )
```

```python
import jax
import jax.numpy as jnp
from jax import lax
from jax.experimental import pallas as pl
from jax.experimental.pallas import tpu as pltpu
from jax.sharding import Mesh, PartitionSpec as P

beta_one = 0.9
beta_two = 0.999
bias_one = 1.0 - 0.9**10
bias_two = 1.0 - 0.999**10
epsilon = 1e-08
decay_rate = 0.1
max_norm = 1.0

AXES = ("yl", "xa", "xb", "z", "yh", "c")
SIZES = (2, 2, 2, 8, 2, 2)
NZ = 8
OWN = 48
WIDTH = 768
D = 3072
TOK = 256
F32 = jnp.float32
BF16 = jnp.bfloat16


def index_of(yl, x, z, yh, c):
    return (((yl * 4 + x) * 8 + z) * 2 + yh) * 2 + c


def pairs(move):
    out = []
    for yl in range(2):
        for x in range(4):
            for z in range(8):
                for yh in range(2):
                    for c in range(2):
                        out.append((index_of(yl, x, z, yh, c), index_of(*move(yl, x, z, yh, c))))
    return out


SWAP_CORE = pairs(lambda yl, x, z, yh, c: (yl, x, z, yh, 1 - c))
SWAP_YH = pairs(lambda yl, x, z, yh, c: (yl, x, z, 1 - yh, c))
SWAP_YL = pairs(lambda yl, x, z, yh, c: (1 - yl, x, z, yh, c))
X_UP = pairs(lambda yl, x, z, yh, c: (yl, (x + 1) % 4, z, yh, c))
X_DOWN = pairs(lambda yl, x, z, yh, c: (yl, (x - 1) % 4, z, yh, c))
X_FAR = pairs(lambda yl, x, z, yh, c: (yl, (x + 2) % 4, z, yh, c))
Z_UP = pairs(lambda yl, x, z, yh, c: (yl, x, (z + 1) % 8, yh, c))
Z_DOWN = pairs(lambda yl, x, z, yh, c: (yl, x, (z - 1) % 8, yh, c))


def send(value, perm):
    return lax.ppermute(value, AXES, perm)


def gather(value, axes, n):
    copies = jnp.broadcast_to(value[None], (n,) + value.shape)
    return lax.all_to_all(copies, axes, 0, 0, tiled=True)


def after(value, *earlier):
    return lax.optimization_barrier((value,) + earlier)[0]


def add(*terms):
    total = terms[0].astype(F32)
    for term in terms[1:]:
        total = total + term.astype(F32)
    return total


VMEM_LIMIT = 28 * 1024 * 1024
ALL_VMEM = 60 * 1024 * 1024


def grad_kernel(b0, b1, b2, b3, og, out, blocks):
    for k, block in enumerate((b0, b1, b2, b3)):
        blocks[k * TOK : (k + 1) * TOK, :] = block[...]
    total = lax.dot_general(blocks[...], og[...], (((0,), (0,)), ((), ())), preferred_element_type=F32)
    out[...] = total.astype(BF16).reshape(2, 1, 1, NZ, OWN, WIDTH)


def weight_grad(blocks, og):
    tile = 768
    return pl.pallas_call(
        grad_kernel,
        grid=(D // tile,),
        in_specs=[pl.BlockSpec((TOK, tile), lambda i: (0, i))] * 4 + [pl.BlockSpec((4 * TOK, WIDTH), lambda i: (0, 0))],
        out_specs=pl.BlockSpec((2, 1, 1, NZ, OWN, WIDTH), lambda i: (0, i // 2, lax.rem(i, 2), 0, 0, 0)),
        scratch_shapes=[pltpu.VMEM((4 * TOK, tile), BF16)],
        out_shape=jax.ShapeDtypeStruct((2, 2, 2, NZ, OWN, WIDTH), BF16),
        compiler_params=pltpu.CompilerParams(vmem_limit_bytes=VMEM_LIMIT),
        cost_estimate=pl.CostEstimate(flops=8 * TOK * WIDTH * D, bytes_accessed=16 * 1024 * 1024, transcendentals=0),
        name="weight_grad",
    )(*blocks, og)


def stream_kernel(here, og, *refs):
    lanes, (p0, p1, p2, p3, rows) = (refs[:9], refs[9:18]), refs[18:]
    step = pl.program_id(0)
    yl = lax.rem(step // 2 - here[0] + 2, 2)
    for lane, blocks in enumerate(lanes):

        @pl.when(yl == lane)
        def _():
            for k in range(2):
                x = lax.rem(lax.rem(step, 2) * 2 + k - here[1] + 4, 4)
                for z, block in zip((0, 1, 2, 3, 5, 6, 7), blocks):
                    rows[k, lax.rem(here[2] + z, NZ)] = block[x]
                far = jnp.where(x < 2, blocks[7][jnp.minimum(x, 1)], blocks[8][jnp.maximum(x - 2, 0)])
                rows[k, lax.rem(here[2] + 4, NZ)] = far

    full = rows[...].reshape(2 * NZ * OWN, WIDTH)
    for k, out in enumerate((p0, p1, p2, p3)):
        out[...] = lax.dot_general(
            og[k * TOK : (k + 1) * TOK, :], full, (((1,), (1,)), ((), ())), preferred_element_type=F32
        ).astype(BF16)


def stream_parts(here, og, blocks):
    tile = 2 * NZ * OWN
    whole = [pl.BlockSpec((n, OWN, WIDTH), lambda i, here: (0, 0, 0)) for n in (4, 4, 4, 4, 4, 4, 4, 2, 2) * 2]
    return pl.pallas_call(
        stream_kernel,
        grid_spec=pltpu.PrefetchScalarGridSpec(
            num_scalar_prefetch=1,
            grid=(4,),
            in_specs=[pl.BlockSpec((4 * TOK, WIDTH), lambda i, here: (0, 0))] + whole,
            out_specs=[pl.BlockSpec((TOK, tile), lambda i, here: (0, i))] * 4,
            scratch_shapes=[pltpu.VMEM((2, NZ, OWN, WIDTH), BF16)],
        ),
        out_shape=[jax.ShapeDtypeStruct((TOK, D), BF16)] * 4,
        compiler_params=pltpu.CompilerParams(vmem_limit_bytes=ALL_VMEM),
        cost_estimate=pl.CostEstimate(flops=8 * TOK * WIDTH * D, bytes_accessed=16 * 1024 * 1024, transcendentals=0),
        name="stream_parts",
    )(here, og, *blocks)


def body(block_out, gate, out_grad, zero_weight, first_moment, second_moment):
    here = jnp.stack([lax.axis_index("yl"), lax.axis_index(("xa", "xb")), lax.axis_index("z")]).astype(jnp.int32)
    ti = lax.axis_index("yh") * 2 + lax.axis_index("c")

    order = [lax.dynamic_slice_in_dim(out_grad, lax.bitwise_xor(ti, k) * TOK, TOK, 0) for k in range(4)]
    out_grad = jnp.concatenate(order)

    with jax.named_scope("start"):
        far = send(block_out, SWAP_YH)
        weight = zero_weight.astype(BF16)
        lane_0 = jnp.stack([weight, send(weight, X_DOWN), send(weight, X_FAR), send(weight, X_UP)])
        near = send(block_out, SWAP_CORE)
        lane_0, near = lax.optimization_barrier((lane_0, near))
        lane_1 = send(lane_0, SWAP_YL)

    def ring(up, down):
        return send(up, Z_UP), send(down, Z_DOWN)

    with jax.named_scope("weight_gather"):
        first_0 = ring(lane_0, lane_0)
        second_0 = ring(*first_0)
        third_0 = ring(*second_0)
        far, out_grad, third_0 = lax.optimization_barrier((far, out_grad, third_0))
        fourth_0 = ring(third_0[0][:2], third_0[1][2:])
        first_1 = ring(lane_1, lane_1)

    with jax.named_scope("weight_grad"):
        far_near = send(far, SWAP_CORE)
        grad = weight_grad((block_out, near, far, far_near), out_grad)

    with jax.named_scope("grad_scatter"):
        got = lax.all_to_all(grad.reshape(8, NZ, OWN, WIDTH), ("xb", "yl", "xa"), 0, 0, tiled=True)

    with jax.named_scope("weight_gather"):
        first_1, fourth_0 = lax.optimization_barrier((first_1, fourth_0, grad))[:2]
        second_1 = ring(*first_1)
        third_1 = ring(*second_1)
        fourth_1 = ring(third_1[0][:2], third_1[1][2:])

    with jax.named_scope("stream"):
        blocks = []
        for lane, (up, down), (up2, down2), (up3, down3), fourth in (
            (lane_0, first_0, second_0, third_0, fourth_0),
            (lane_1, first_1, second_1, third_1, fourth_1),
        ):
            blocks += [lane, down, down2, down3, up3, up2, up, *fourth]
        p0, p1, p2, p3 = stream_parts(here, out_grad, blocks)
        r3, r1 = send(p3, SWAP_CORE), send(p1, SWAP_CORE)
        s2 = add(p2, r3).astype(BF16)
        s2, r1 = lax.optimization_barrier((s2, r1))
        q2 = send(s2, SWAP_YH)

    with jax.named_scope("grad_scatter"):
        total = add(*got).astype(BF16)
        owner_grad = add(*lax.all_to_all(total, ("z",), 0, 0, tiled=True))

    with jax.named_scope("norm"):
        local = jnp.sum(owner_grad * owner_grad)
        local = gather(jnp.full((1, 128), local, F32), ("yl", "xa", "xb", "yh", "c"), 32)
        stream = add(p0, r1, q2)
        stream_out = stream.astype(BF16)
        branch_out = (gate * stream).astype(BF16)
        local, stream_out, branch_out = lax.optimization_barrier((local, stream_out, branch_out))
        local = jnp.sum(local.reshape(32, 128), axis=0, keepdims=True)
        norm_sq = jnp.sum(gather(local, ("z",), 8), axis=0)[:1, :1]

    factor = jnp.minimum(1.0, max_norm / (jnp.sqrt(norm_sq) + 1e-06))
    clipped = factor * owner_grad
    first = beta_one * first_moment + (1.0 - beta_one) * clipped
    second = beta_two * second_moment + (1.0 - beta_two) * clipped * clipped
    update = first / bias_one / (jnp.sqrt(second / bias_two) + epsilon) + decay_rate * zero_weight
    return (stream_out, branch_out, update)


def solution(mesh):
    fine = Mesh(mesh.devices.reshape(SIZES), AXES)
    dp, tensor = ("yl", "xa", "xb", "z"), ("yh", "c")
    placed = (P(AXES, None), P(dp, None), P(dp, tensor), P(dp, tensor), P(dp, tensor), P(dp, tensor))
    return jax.shard_map(
        body,
        mesh=fine,
        in_specs=placed,
        out_specs=(P(AXES, None), P(AXES, None), P(dp, tensor)),
        check_vma=False,
    )
```
